32 devices in a mesh: row: 8 (over y, x, core), col: 4 (over z).
Axes of the slice: x: 2, y: 2, z: 4, core: 2. Of those that a mesh axis runs over, the one named last changes fastest.
Arguments:
- features: bfloat16 [8192, 256], P(('row', 'col')), may hold values from -6 to 6
- out_degree: int32 [8192], P('row'), may hold values from 8 to 1024
- in_degree: int32 [8192], P('col'), may hold values from 8 to 1024
- tile_blocks: int32 [8, 4, 2, 128], P('row', 'col'), may hold values from 0 to 15, as said below
- tile_count: int32 [8, 4], P('row', 'col'), may hold values from 16 to 128, as said below
- tile_weights: bfloat16 [8, 4, 128, 128, 128], P('row', 'col'), may hold values from 0 to 4, as said below
- weight: bfloat16 [256, 256], replicated, may hold values from -0.375 to 0.375
- cotangent: bfloat16 [8192, 256], P(('col', 'row')), may hold values from -6 to 6
Outputs:
- hidden: bfloat16 [8192, 256], P(('col', 'row'))
- input_grad: bfloat16 [8192, 256], P(('row', 'col'))
- weight_grad: float32 [256, 256], replicated
The draws below stay inside these ranges and needn't reach their ends.
Inputs may be any that keep to these rules, and one draw needn't show every extreme that they name: `tile_blocks`: entry [r, c, 0, s] is a target block below 16, entry [r, c, 1, s] a source block below 8; the pairs of one device position are distinct. `tile_count`: live tile slots of a device position are its first ones; some position has exactly 128. `tile_weights`: Non-negative edge weights.
All inputs are finite; a program needn't handle non-finite values.
Results may differ from the reference program's by a relative error of at most 0.0067.
Values may be sent and summed in bfloat16 or wider, within the bound.
A program may use at most 192 MiB of HBM per device.

```python
import jax
import jax.numpy as jnp
from jax import lax

HID = 256
TILE = 128
NODE_DEV = 256
TILE_CAP = 128
NODES = 8192
SRC_BLOCKS = 8
TGT_BLOCKS = 16
N_ROW = 8
N_COL = 4


def draw_tile_blocks(key, part):
    region = TGT_BLOCKS * SRC_BLOCKS

    def one_device(index):
        order = jax.random.permutation(jax.random.fold_in(key, index), region)[:TILE_CAP]
        return jnp.stack([order // SRC_BLOCKS, order % SRC_BLOCKS]).astype(jnp.int32)
    picked = jax.vmap(one_device)(jnp.arange(N_ROW * N_COL))
    return picked.reshape(N_ROW, N_COL, 2, TILE_CAP)


def draw_tile_count(key, part):
    positions = N_ROW * N_COL
    base = jax.random.randint(jax.random.fold_in(key, 11), (positions,), max(1, TILE_CAP // 8), TILE_CAP // 2 + 1)
    busiest = jax.random.randint(jax.random.fold_in(key, 12), (), 0, positions)
    filled = jnp.where(jnp.arange(positions) == busiest, TILE_CAP, base)
    return filled.astype(jnp.int32).reshape(N_ROW, N_COL)


def draw_tile_weights(key, part):
    shape = (N_ROW, N_COL, TILE_CAP, TILE, TILE)
    kept = jax.random.bernoulli(jax.random.fold_in(key, 21), 0.5, shape)
    values = jax.random.uniform(jax.random.fold_in(key, 22), shape, jnp.float32, 0.5, 2.0)
    return jnp.where(kept, values, 0.0).astype(jnp.float32).astype(jnp.bfloat16)


def plant(drawn, key, low, high):
    index_at = [jax.random.randint(jax.random.fold_in(key, axis), (), 0, length) for axis, length in enumerate(drawn.shape)]
    widest = drawn.shape.index(max(drawn.shape))
    next_to = index_at[:widest] + [(index_at[widest] + 1) % drawn.shape[widest]] + index_at[widest + 1:]
    return drawn.at[tuple(index_at)].set(low).at[tuple(next_to)].set(high)


def block_scale(rng, dims, split, low, top_value):
    gain = 1.0
    for position, shards_of in split:
        draws = jax.random.uniform(jax.random.fold_in(jax.random.fold_in(rng, 6), position), (shards_of,), jnp.float32, low / len(split), top_value / len(split))
        gain = gain * jnp.repeat(jnp.exp(draws), dims[position] // shards_of).reshape((-1,) + (1,) * (len(dims) - 1 - position))
    return gain


def scatter_about(key, dims, scale, reach, pieces=(), dtype=jnp.bfloat16):
    gain = block_scale(key, dims, pieces, -0.22, 0.18) if pieces else 1.0
    values = jax.random.normal(key, dims, jnp.float32) * scale * gain
    return jnp.minimum(jnp.maximum(values, -reach), reach).astype(dtype)


def setup_inputs(seed: int = 0) -> dict:
    key_list = jax.random.split(jax.random.key(seed), 9)
    return {
        "features": scatter_about(key_list[0], (NODES, HID), 1.0, 6.0, ((0, 32),)),
        "out_degree": plant(jax.random.randint(key_list[1], (NODES,), 8, 1025), jax.random.fold_in(key_list[1], 1), 8, 1024).astype(jnp.int32),
        "in_degree": plant(jax.random.randint(key_list[2], (NODES,), 8, 1025), jax.random.fold_in(key_list[2], 1), 8, 1024).astype(jnp.int32),
        "tile_blocks": draw_tile_blocks(jax.random.fold_in(key_list[8], 71), 0),
        "tile_count": draw_tile_count(jax.random.fold_in(key_list[8], 71), 0),
        "tile_weights": draw_tile_weights(jax.random.fold_in(key_list[8], 71), 0),
        "weight": scatter_about(key_list[6], (HID, HID), HID ** -0.5, 0.375),
        "cotangent": scatter_about(key_list[7], (NODES, HID), 1.0, 6.0, ((0, 32),)),
    }


def silu_slope(pre_act):
    gate_sig = jax.nn.sigmoid(pre_act)
    return gate_sig * (1.0 + pre_act * (1.0 - gate_sig))

def reference(features, out_degree, in_degree, tile_blocks, tile_count, tile_weights, weight, cotangent):
    feat_width = features.shape[1]
    src_len = NODE_DEV * N_COL
    tgt_len = NODE_DEV * N_ROW
    out_scale = lax.rsqrt(out_degree.astype(jnp.float32))
    in_scale = lax.rsqrt(in_degree.astype(jnp.float32))
    src_scaled = (features.astype(jnp.float32) * out_scale[:, None]).astype(jnp.bfloat16)

    def device_tiles(device_at):
        row_at = (device_at // N_COL).astype(jnp.int32)
        col_at = (device_at % N_COL).astype(jnp.int32)
        blocks = tile_blocks[row_at, col_at]
        is_live = (jnp.arange(TILE_CAP) < tile_count[row_at, col_at]).astype(jnp.float32)
        tile_vals = tile_weights[row_at, col_at].astype(jnp.float32) * is_live[:, None, None]
        return (row_at, col_at, blocks, tile_vals)

    def forward_step(device_at, totals):
        row_at, col_at, blocks, tile_vals = device_tiles(device_at)
        source = lax.dynamic_slice_in_dim(src_scaled, row_at * src_len, src_len, 0)
        source = source.reshape(SRC_BLOCKS, TILE, feat_width)
        picked = source[blocks[1]].astype(jnp.float32)
        products = jnp.einsum('trc,tch->trh', tile_vals, picked)
        partial_value = jax.ops.segment_sum(products, blocks[0], num_segments=TGT_BLOCKS)
        return totals.at[col_at].add(partial_value.reshape(tgt_len, feat_width))
    totals = lax.fori_loop(0, N_ROW * N_COL, forward_step, jnp.zeros((N_COL, tgt_len, feat_width), jnp.float32))
    agg_rows = (totals.reshape(NODES, feat_width) * in_scale[:, None]).astype(jnp.bfloat16)
    pre_act = jnp.dot(agg_rows, weight, preferred_element_type=jnp.float32)
    hidden = jax.nn.silu(pre_act).astype(jnp.bfloat16)
    pre_grad = (cotangent.astype(jnp.float32) * silu_slope(pre_act)).astype(jnp.bfloat16)
    weight_grad = jnp.dot(agg_rows.T, pre_grad, preferred_element_type=jnp.float32)
    back_rows = jnp.dot(pre_grad, weight.T, preferred_element_type=jnp.float32)
    target_grad = (back_rows * in_scale[:, None]).astype(jnp.bfloat16)

    def backward_step(device_at, totals):
        row_at, col_at, blocks, tile_vals = device_tiles(device_at)
        target = lax.dynamic_slice_in_dim(target_grad, col_at * tgt_len, tgt_len, 0)
        target = target.reshape(TGT_BLOCKS, TILE, feat_width)
        picked = target[blocks[0]].astype(jnp.float32)
        products = jnp.einsum('trc,trh->tch', tile_vals, picked)
        partial_value = jax.ops.segment_sum(products, blocks[1], num_segments=SRC_BLOCKS)
        return totals.at[row_at].add(partial_value.reshape(src_len, feat_width))
    src_totals = lax.fori_loop(0, N_ROW * N_COL, backward_step, jnp.zeros((N_ROW, src_len, feat_width), jnp.float32))
    input_grad = (src_totals.reshape(NODES, feat_width) * out_scale[:, None]).astype(jnp.bfloat16)
    return (hidden, input_grad, weight_grad)
```

```python
import functools

import jax
import jax.numpy as jnp
from jax import lax
from jax.experimental import pallas as pl
from jax.experimental.pallas import tpu as pltpu
from jax.sharding import PartitionSpec as P

TILE = 128
F32 = jnp.float32
BF16 = jnp.bfloat16
MESH = pl.DeviceIdType.MESH


def bit_orders(nr):
    bits = nr.bit_length() - 1
    return ([0] + list(range(1, bits)), [0] + list(range(bits - 1, 0, -1)))


class Group:
    def __init__(self, nr, me):
        self.nr, self.me = nr, me
        self.orders = bit_orders(nr)
        self.stages = len(self.orders[0])
        self.base = [nr - (nr >> s) for s in range(self.stages)]

    def bit(self, value, k):
        return (value // (1 << k)) % 2

    def partner(self, k):
        return self.me + (1 << k) * (1 - 2 * self.bit(self.me, k))

    def slot(self, half, stage, piece):
        rest = self.orders[half][stage + 1:]
        return self.base[stage] + sum(
            (self.bit(piece, b) * (1 << i) for i, b in enumerate(rest)), 0
        )

    def pieces(self, half, stage, mine):
        order = self.orders[half]
        own = sum((self.bit(self.me, b) * (1 << b) for b in order[:stage]), 0)
        k = order[stage]
        here = self.bit(self.me, k)
        here = here if mine else 1 - here
        rest = order[stage + 1:]
        return [
            own + here * (1 << k) + sum(((j >> i) & 1) << b for i, b in enumerate(rest))
            for j in range(1 << len(rest))
        ]


def kernel(
    nr, nc,
    feat_ref, odeg_ref, ideg_ref, blocks_ref, count_ref, tiles_hbm, w_ref, cot_ref,
    hid_ref, ig_ref, wg_ref,
    tiles, adj, adj_t, table_v, table_s, src, part, rs_out, rs_in, tg, zq_out, zq_in,
    wga_out, wga_in, wgb_in, wgc_in,
    loc_sem, tab_sem, zs_send, zs_recv, rs_send, rs_recv, ag_send, ag_recv,
    zq_send, zq_recv, wa_send, wa_recv, wb_send, wb_recv, wc_send, wc_recv,
):
    rows, hid = feat_ref.shape
    half_w = hid // 2
    sb, tb = nc * rows // TILE, nr * rows // TILE
    slots = tiles.shape[0]
    me_r, me_c = lax.axis_index("row"), lax.axis_index("col")
    group = Group(nr, me_r)
    row_id = lambda r: {"row": r, "col": me_c}
    col_id = lambda c: {"row": me_r, "col": c}

    def remote(src_ref, dst_ref, send, recv, where):
        return pltpu.make_async_remote_copy(
            src_ref=src_ref, dst_ref=dst_ref, send_sem=send, recv_sem=recv,
            device_id=where, device_id_type=MESH,
        )

    load_tiles = pltpu.make_async_copy(tiles_hbm, tiles, loc_sem)
    load_tiles.start()

    barrier = pltpu.get_barrier_semaphore()
    for d in range(1, nr):
        pl.semaphore_signal(
            barrier, inc=1, device_id=row_id(lax.rem(me_r + d, nr)), device_id_type=MESH
        )
    for d in range(1, nc):
        pl.semaphore_signal(
            barrier, inc=1, device_id=col_id(lax.rem(me_c + d, nc)), device_id_type=MESH
        )

    def scale_rows(deg_ref, first):
        cols = []
        for h in range(rows // TILE):
            deg = deg_ref[pl.ds(first + h, 1), :]
            line = lax.rsqrt(deg.astype(F32))
            cols.append(jnp.broadcast_to(line, (TILE, TILE)).T)
        return jnp.concatenate(cols, axis=0)

    out_scale = scale_rows(odeg_ref, me_c * (rows // TILE))
    for h in range(2):
        cut = slice(h * half_w, (h + 1) * half_w)
        src[h, me_c] = (feat_ref[:, cut].astype(F32) * out_scale).astype(BF16)

    pl.semaphore_wait(barrier, nr + nc - 2)

    def gather_copy(h, block, right):
        to = me_c + 1 if right else me_c - 1
        return remote(
            src.at[h, block], src.at[h, block],
            zs_send.at[0 if right else 1, h, block], zs_recv.at[h, block], col_id(to),
        )

    def gather_cases(k, right):
        block = me_c - k if right else me_c + k
        there = block >= 0 if right else block < nc
        on = me_c + 1 < nc if right else me_c >= 1
        return block, there, on

    def gather_step(k, h):
        for right in (True, False):
            block, there, on = gather_cases(k, right)
            if k > 0:
                @pl.when(there)
                def _():
                    gather_copy(h, block, right).wait_recv()
            if k < nc - 1:
                @pl.when(jnp.logical_and(there, on))
                def _():
                    gather_copy(h, block, right).start()

    def gather_drain(h):
        for k in range(nc - 1):
            for right in (True, False):
                block, there, on = gather_cases(k, right)

                @pl.when(jnp.logical_and(there, on))
                def _():
                    gather_copy(h, block, right).wait_send()

    for h in range(2):
        gather_step(0, h)

    flat = blocks_ref[0:1, :] * sb + blocks_ref[1:2, :]
    slot_line = lax.broadcasted_iota(jnp.int32, (1, slots), 1)
    flat = jnp.where(slot_line < count_ref[0, 0], flat, -1)
    down = jnp.broadcast_to(flat.astype(F32), (slots, slots)).T.astype(jnp.int32)
    slot_down = lax.broadcasted_iota(jnp.int32, (slots, slots), 0)
    lane = lax.broadcasted_iota(jnp.int32, (slots, slots), 1)
    for g in range(table_v.shape[0]):
        found = jnp.where(down == lane + g * slots, slot_down, -1)
        table_v[g:g + 1, :] = jnp.max(found, axis=0, keepdims=True)
    to_smem = pltpu.make_async_copy(table_v, table_s, tab_sem)
    to_smem.start()
    to_smem.wait()
    load_tiles.wait()

    def densify(t, carry):
        for s in range(sb):
            at = t * sb + s
            slot = table_s[at // slots, at % slots]
            tile = tiles[jnp.maximum(slot, 0)]
            tile = jnp.where(slot >= 0, tile, jnp.zeros_like(tile))
            adj[pl.ds(t * TILE, TILE), s * TILE:(s + 1) * TILE] = tile
            adj_t[t, s * TILE:(s + 1) * TILE, :] = tile.T
        return carry

    lax.fori_loop(0, tb, densify, 0)

    for k in range(1, nc):
        for h in range(2):
            gather_step(k, h)

    def rs_copy(h, stage, piece):
        slot = group.slot(h, stage, piece)
        return remote(
            rs_out.at[h, piece], rs_in.at[h, slot], rs_send.at[h, slot], rs_recv.at[h, slot],
            row_id(group.partner(group.orders[h][stage])),
        )

    def target_sums(piece):
        block = adj[pl.ds(pl.multiple_of(piece * rows, rows), rows), :]
        return [
            jnp.dot(block, src[h].reshape(nc * rows, half_w), preferred_element_type=F32)
            for h in range(2)
        ]

    for piece in group.pieces(0, 0, False):
        sums = target_sums(piece)
        for h in range(2):
            rs_out[h, piece] = sums[h].astype(BF16)
            rs_copy(h, 0, piece).start()
    for piece in group.pieces(0, 0, True):
        sums = target_sums(piece)
        for h in range(2):
            part[h, piece] = sums[h]

    for stage in range(1, group.stages):
        for h in range(2):
            for piece in group.pieces(h, stage, False):
                rs_copy(h, stage - 1, piece).wait_recv()
                got = rs_in[h, group.slot(h, stage - 1, piece)].astype(F32)
                rs_out[h, piece] = (part[h, piece] + got).astype(BF16)
                rs_copy(h, stage, piece).start()
        for h in range(2):
            for piece in group.pieces(h, stage, True):
                rs_copy(h, stage - 1, piece).wait_recv()
                got = rs_in[h, group.slot(h, stage - 1, piece)].astype(F32)
                part[h, piece] = part[h, piece] + got

    in_scale = scale_rows(ideg_ref, me_r * (rows // TILE))
    last = group.stages - 1
    totals = []
    for h in range(2):
        rs_copy(h, last, me_r).wait_recv()
        got = rs_in[h, group.slot(h, last, me_r)].astype(F32)
        totals.append(((part[h, me_r] + got) * in_scale).astype(BF16))
    agg = jnp.concatenate(totals, axis=1)
    pre_act = jnp.dot(agg, w_ref[...], preferred_element_type=F32)
    gate = jax.nn.sigmoid(pre_act)
    hid_ref[...] = (pre_act * gate).astype(BF16)
    slope = gate * (1.0 + pre_act * (1.0 - gate))
    pre_grad = (cot_ref[...].astype(F32) * slope).astype(BF16)
    back = lax.dot_general(
        pre_grad, w_ref[...], (((1,), (1,)), ((), ())), preferred_element_type=F32
    )

    def ag_copy(h, stage, piece):
        slot = group.slot(h, stage, piece)
        return remote(
            tg.at[h, piece], tg.at[h, piece], ag_send.at[h, slot], ag_recv.at[h, slot],
            row_id(group.partner(group.orders[h][stage])),
        )

    for h in range(2):
        tg[h, me_r] = (back[:, h * half_w:(h + 1) * half_w] * in_scale).astype(BF16)
        for stage in reversed(range(group.stages)):
            ag_copy(h, stage, me_r).start()

    wg_part = lax.dot_general(
        agg, pre_grad, (((0,), (0,)), ((), ())), preferred_element_type=F32
    )
    piece_rows = hid // nr
    wga_out[...] = wg_part.astype(BF16).reshape(nr, piece_rows, hid)

    def wa_copy(d):
        to = lax.rem(me_r + d, nr)
        return remote(
            wga_out.at[to], wga_in.at[d], wa_send.at[d], wa_recv.at[d], row_id(to)
        )

    def wb_copy(d):
        to = lax.rem(me_c + d, nc)
        return remote(
            wgb_in.at[me_c], wgb_in.at[me_c], wb_send.at[d], wb_recv.at[d], col_id(to)
        )

    def wb_arrival(d):
        frm = lax.rem(me_c + nc - d, nc)
        return remote(
            wgb_in.at[frm], wgb_in.at[frm], wb_send.at[d], wb_recv.at[d],
            col_id(lax.rem(me_c + d, nc)),
        )

    def wc_copy(d):
        to = lax.rem(me_r + d, nr)
        return remote(
            wgc_in.at[me_r], wgc_in.at[me_r], wc_send.at[d], wc_recv.at[d], row_id(to)
        )

    def wc_arrival(d):
        frm = lax.rem(me_r + nr - d, nr)
        return remote(
            wgc_in.at[frm], wgc_in.at[frm], wc_send.at[d], wc_recv.at[d],
            row_id(lax.rem(me_r + d, nr)),
        )

    def ag_receive(h, stage, piece):
        ag_copy(h, stage, piece).wait_recv()
        for onward in reversed(range(stage)):
            ag_copy(h, onward, piece).start()

    for stage in reversed(range(1, group.stages)):
        for h in range(2):
            for piece in group.pieces(h, stage, False):
                ag_receive(h, stage, piece)

    for d in range(1, nr):
        wa_copy(d).start()

    for h in range(2):
        for piece in group.pieces(h, 0, False):
            ag_receive(h, 0, piece)

    def zq_copy(h, dest, right):
        way = 0 if right else 1
        return remote(
            zq_out.at[h, dest], zq_in.at[way, h, dest], zq_send.at[h, dest],
            zq_recv.at[way, h, dest], col_id(me_c + 1 if right else me_c - 1),
        )

    def source_sums(dest):
        total = None
        at = pl.ds(pl.multiple_of(dest * rows, rows), rows)
        block = jnp.concatenate([adj_t[t, at, :] for t in range(tb)], axis=1)
        return [
            jnp.dot(block, tg[h].reshape(nr * rows, half_w), preferred_element_type=F32)
            for h in range(2)
        ]

    def stream(m, right):
        dest = me_c + m if right else me_c - m
        ok = dest < nc if right else dest >= 0
        upstream = me_c >= 1 if right else me_c + 1 < nc
        way = 0 if right else 1

        @pl.when(ok)
        def _():
            sums = source_sums(dest)
            for h in range(2):
                zq_out[h, dest] = sums[h].astype(BF16)

                @pl.when(upstream)
                def _():
                    zq_copy(h, dest, right).wait_recv()
                    got = zq_in[way, h, dest].astype(F32)
                    zq_out[h, dest] = (sums[h] + got).astype(BF16)

                zq_copy(h, dest, right).start()

    for m in range(nc - 1, 0, -1):
        for right in (True, False):
            stream(m, right)

    for d in range(1, nr):
        wa_copy(d).wait_recv()
    own = wga_out[me_r].astype(F32)
    for d in range(1, nr):
        own = own + wga_in[d].astype(F32)
    wgb_in[me_c] = own
    for d in range(1, nc):
        wb_copy(d).start()

    own_sums = source_sums(me_c)

    for d in range(1, nc):
        wb_arrival(d).wait_recv()
    total = wgb_in[0]
    for c in range(1, nc):
        total = total + wgb_in[c]
    wgc_in[me_r] = total
    for d in range(1, nr):
        wc_copy(d).start()

    for h in range(2):
        part[h, 0] = own_sums[h]
        for right in (True, False):
            there = me_c >= 1 if right else me_c + 1 < nc
            way = 0 if right else 1

            @pl.when(there)
            def _():
                zq_copy(h, me_c, right).wait_recv()
                part[h, 0] = part[h, 0] + zq_in[way, h, me_c].astype(F32)

        ig_ref[:, h * half_w:(h + 1) * half_w] = (part[h, 0] * out_scale).astype(BF16)

    for d in range(1, nr):
        wc_arrival(d).wait_recv()
    wg_ref[...] = wgc_in[...].reshape(hid, hid)

    for h in range(2):
        gather_drain(h)
        for stage in range(group.stages):
            for piece in group.pieces(h, stage, False):
                rs_copy(h, stage, piece).wait_send()
            for piece in group.pieces(h, stage, True):
                ag_copy(h, stage, piece).wait_send()
        for m in range(1, nc):
            @pl.when(me_c + m < nc)
            def _():
                zq_copy(h, me_c + m, True).wait_send()

            @pl.when(me_c - m >= 0)
            def _():
                zq_copy(h, me_c - m, False).wait_send()
    for d in range(1, nr):
        wa_copy(d).wait_send()
        wc_copy(d).wait_send()
    for d in range(1, nc):
        wb_copy(d).wait_send()


def shards(
    nr, nc,
    features, out_degree, in_degree, tile_blocks, tile_count, tile_weights, weight, cotangent
):
    rows, hid = features.shape
    half_w = hid // 2
    slots = tile_weights.shape[2]
    src_rows, tgt_rows = out_degree.shape[0], in_degree.shape[0]
    sb, tb = src_rows // TILE, tgt_rows // TILE
    vmem = pl.BlockSpec(memory_space=pltpu.VMEM)
    smem = pl.BlockSpec(memory_space=pltpu.SMEM)
    dma = pltpu.SemaphoreType.DMA
    table_rows = -(-sb * tb // slots)
    return pl.pallas_call(
        functools.partial(kernel, nr, nc),
        out_shape=(
            jax.ShapeDtypeStruct((rows, hid), BF16),
            jax.ShapeDtypeStruct((rows, hid), BF16),
            jax.ShapeDtypeStruct((hid, hid), F32),
        ),
        in_specs=[
            vmem, vmem, vmem, vmem, smem, pl.BlockSpec(memory_space=pl.ANY), vmem, vmem
        ],
        out_specs=(vmem, vmem, vmem),
        scratch_shapes=[
            pltpu.VMEM((slots, TILE, TILE), BF16),
            pltpu.VMEM((tgt_rows, src_rows), BF16),
            pltpu.VMEM((tb, src_rows, TILE), BF16),
            pltpu.VMEM((table_rows, slots), jnp.int32),
            pltpu.SMEM((table_rows, slots), jnp.int32),
            pltpu.VMEM((2, nc, rows, half_w), BF16),
            pltpu.VMEM((2, nr, rows, half_w), F32),
            pltpu.VMEM((2, nr, rows, half_w), BF16),
            pltpu.VMEM((2, nr - 1, rows, half_w), BF16),
            pltpu.VMEM((2, nr, rows, half_w), BF16),
            pltpu.VMEM((2, nc, rows, half_w), BF16),
            pltpu.VMEM((2, 2, nc, rows, half_w), BF16),
            pltpu.VMEM((nr, hid // nr, hid), BF16),
            pltpu.VMEM((nr, hid // nr, hid), BF16),
            pltpu.VMEM((nc, hid // nr, hid), F32),
            pltpu.VMEM((nr, hid // nr, hid), F32),
            dma, dma,
            dma((2, 2, nc)), dma((2, nc)),
            dma((2, nr - 1)), dma((2, nr - 1)),
            dma((2, nr - 1)), dma((2, nr - 1)),
            dma((2, nc)), dma((2, 2, nc)),
            dma((nr,)), dma((nr,)),
            dma((nc,)), dma((nc,)),
            dma((nr,)), dma((nr,)),
        ],
        compiler_params=pltpu.CompilerParams(
            collective_id=0, has_side_effects=True, vmem_limit_bytes=60 * 1024 * 1024
        ),
    )(
        features,
        out_degree.reshape(sb, TILE),
        in_degree.reshape(tb, TILE),
        tile_blocks[0, 0],
        tile_count,
        tile_weights[0, 0],
        weight,
        cotangent,
    )


def solution(mesh):
    nr, nc = mesh.shape["row"], mesh.shape["col"]
    placed = (
        P(("row", "col"), None),
        P("row"),
        P("col"),
        P("row", "col", None, None),
        P("row", "col"),
        P("row", "col", None, None, None),
        P(),
        P(("col", "row"), None),
    )
    return jax.shard_map(
        functools.partial(shards, nr, nc),
        mesh=mesh,
        in_specs=placed,
        out_specs=(P(("col", "row"), None), P(("row", "col"), None), P()),
        check_vma=False,
    )
```

```python
import functools

import jax
import jax.numpy as jnp
from jax import lax
from jax.experimental import pallas as pl
from jax.experimental.pallas import tpu as pltpu
from jax.sharding import PartitionSpec as P

TILE = 128
F32 = jnp.float32
BF16 = jnp.bfloat16
MESH = pl.DeviceIdType.MESH


def bit_orders(nr):
    bits = nr.bit_length() - 1
    return ([0] + list(range(1, bits)), [0] + list(range(bits - 1, 0, -1)))


class Group:
    def __init__(self, nr, me):
        self.nr, self.me = nr, me
        self.orders = bit_orders(nr)
        self.stages = len(self.orders[0])
        self.base = [nr - (nr >> s) for s in range(self.stages)]

    def bit(self, value, k):
        return (value // (1 << k)) % 2

    def partner(self, k):
        return self.me + (1 << k) * (1 - 2 * self.bit(self.me, k))

    def slot(self, half, stage, piece):
        rest = self.orders[half][stage + 1:]
        return self.base[stage] + sum(
            (self.bit(piece, b) * (1 << i) for i, b in enumerate(rest)), 0
        )

    def pieces(self, half, stage, mine):
        order = self.orders[half]
        own = sum((self.bit(self.me, b) * (1 << b) for b in order[:stage]), 0)
        k = order[stage]
        here = self.bit(self.me, k)
        here = here if mine else 1 - here
        rest = order[stage + 1:]
        return [
            own + here * (1 << k) + sum(((j >> i) & 1) << b for i, b in enumerate(rest))
            for j in range(1 << len(rest))
        ]


def kernel(
    nr, nc,
    feat_hbm, odeg_hbm, ideg_hbm, blocks_hbm, count_hbm, tiles_hbm, w_hbm, cot_hbm,
    hid_hbm, ig_hbm, wg_hbm,
    feat_ref, odeg_ref, ideg_ref, blocks_ref, count_ref, w_ref, cot_ref, hid_ref, ig_ref,
    in_sem, out_sem,
    tiles, adj, adj_t, table_v, table_s, src, part, rs_out, rs_in, tg, zq_out, zq_in, zq_fin,
    wga_out, wga_in, wgb_in, wgc_in,
    loc_sem, tab_sem, zs_send, zs_recv, rs_send, rs_recv, ag_send, ag_recv,
    zq_send, zq_recv, zf_recv, wa_send, wa_recv, wb_send, wb_recv, wc_send, wc_recv,
):
    rows, hid = feat_ref.shape
    half_w = hid // 2
    sb, tb = nc * rows // TILE, nr * rows // TILE
    slots = tiles.shape[0]
    me_r, me_c = lax.axis_index("row"), lax.axis_index("col")
    group = Group(nr, me_r)
    row_id = lambda r: {"row": r, "col": me_c}
    col_id = lambda c: {"row": me_r, "col": c}

    def remote(src_ref, dst_ref, send, recv, where):
        return pltpu.make_async_remote_copy(
            src_ref=src_ref, dst_ref=dst_ref, send_sem=send, recv_sem=recv,
            device_id=where, device_id_type=MESH,
        )

    barrier = pltpu.get_barrier_semaphore()
    for d in range(1, nr):
        pl.semaphore_signal(
            barrier, inc=1, device_id=row_id(lax.rem(me_r + d, nr)), device_id_type=MESH
        )
    for d in range(1, nc):
        pl.semaphore_signal(
            barrier, inc=1, device_id=col_id(lax.rem(me_c + d, nc)), device_id_type=MESH
        )

    loads = [
        pltpu.make_async_copy(a, b, in_sem.at[i])
        for i, (a, b) in enumerate([
            (feat_hbm, feat_ref), (odeg_hbm, odeg_ref), (blocks_hbm, blocks_ref),
            (count_hbm, count_ref), (ideg_hbm, ideg_ref), (w_hbm, w_ref), (cot_hbm, cot_ref),
        ])
    ]
    load_tiles = pltpu.make_async_copy(tiles_hbm, tiles, loc_sem)
    for load in loads:
        load.start()
    load_tiles.start()
    loads[0].wait()
    loads[1].wait()

    def scale_rows(deg_ref, first):
        cols = []
        for h in range(rows // TILE):
            deg = deg_ref[pl.ds(first + h, 1), :]
            line = lax.rsqrt(deg.astype(F32))
            cols.append(jnp.broadcast_to(line, (TILE, TILE)).T)
        return jnp.concatenate(cols, axis=0)

    out_scale = scale_rows(odeg_ref, me_c * (rows // TILE))
    for h in range(2):
        cut = slice(h * half_w, (h + 1) * half_w)
        src[h, me_c] = (feat_ref[:, cut].astype(F32) * out_scale).astype(BF16)

    pl.semaphore_wait(barrier, nr + nc - 2)

    def gather_copy(h, block, hops, right, at):
        to = me_c + hops if right else me_c - hops
        return remote(
            src.at[h, block], src.at[h, block],
            zs_send.at[0 if right else 1, h, at], zs_recv.at[h, block], col_id(to),
        )

    def inside(step, right):
        return me_c + step < nc if right else me_c >= step

    def gather_own(h, act):
        for hops in (2, 1):
            for right in (True, False):
                @pl.when(inside(hops, right))
                def _():
                    act(gather_copy(h, me_c, hops, right, hops - 1))

    def gather_onward(h, k, act):
        for right in (True, False):
            @pl.when(jnp.logical_and(inside(k, not right), inside(1, right)))
            def _():
                act(gather_copy(h, me_c - k if right else me_c + k, 1, right, k))

    def gather_arrived(h, k):
        for right in (True, False):
            @pl.when(inside(k, not right))
            def _():
                gather_copy(h, me_c - k if right else me_c + k, 1, right, k).wait_recv()

    for h in range(2):
        gather_own(h, lambda c: c.start())

    loads[2].wait()
    loads[3].wait()
    flat = blocks_ref[0:1, :] * sb + blocks_ref[1:2, :]
    slot_line = lax.broadcasted_iota(jnp.int32, (1, slots), 1)
    flat = jnp.where(slot_line < count_ref[...], flat, -1)
    down = jnp.broadcast_to(flat.astype(F32), (slots, slots)).T.astype(jnp.int32)
    slot_down = lax.broadcasted_iota(jnp.int32, (slots, slots), 0)
    lane = lax.broadcasted_iota(jnp.int32, (slots, slots), 1)
    for g in range(table_v.shape[0]):
        found = jnp.where(down == lane + g * slots, slot_down, -1)
        table_v[g:g + 1, :] = jnp.max(found, axis=0, keepdims=True)
    to_smem = pltpu.make_async_copy(table_v, table_s, tab_sem)
    to_smem.start()
    to_smem.wait()
    load_tiles.wait()

    def densify(t, carry):
        for s in range(sb):
            at = t * sb + s
            slot = table_s[at // slots, at % slots]
            tile = tiles[jnp.maximum(slot, 0)]
            tile = jnp.where(slot >= 0, tile, jnp.zeros_like(tile))
            adj[pl.ds(t * TILE, TILE), s * TILE:(s + 1) * TILE] = tile
            adj_t[t, s * TILE:(s + 1) * TILE, :] = tile.T
        return carry

    lax.fori_loop(0, tb, densify, 0)

    for k in range(2, nc):
        for h in range(2):
            gather_arrived(h, k)
            gather_onward(h, k, lambda c: c.start())
    for h in range(2):
        gather_arrived(h, 1)

    def rs_copy(h, stage, piece):
        slot = group.slot(h, stage, piece)
        return remote(
            rs_out.at[h, piece], rs_in.at[h, slot], rs_send.at[h, slot], rs_recv.at[h, slot],
            row_id(group.partner(group.orders[h][stage])),
        )

    def target_sums(piece):
        block = adj[pl.ds(pl.multiple_of(piece * rows, rows), rows), :]
        return [
            jnp.dot(block, src[h].reshape(nc * rows, half_w), preferred_element_type=F32)
            for h in range(2)
        ]

    for piece in group.pieces(0, 0, False):
        sums = target_sums(piece)
        for h in range(2):
            rs_out[h, piece] = sums[h].astype(BF16)
            rs_copy(h, 0, piece).start()
    for piece in group.pieces(0, 0, True):
        sums = target_sums(piece)
        for h in range(2):
            part[h, piece] = sums[h]

    for stage in range(1, group.stages):
        for h in range(2):
            for piece in group.pieces(h, stage, False):
                rs_copy(h, stage - 1, piece).wait_recv()
                got = rs_in[h, group.slot(h, stage - 1, piece)].astype(F32)
                rs_out[h, piece] = (part[h, piece] + got).astype(BF16)
                rs_copy(h, stage, piece).start()
        for h in range(2):
            for piece in group.pieces(h, stage, True):
                rs_copy(h, stage - 1, piece).wait_recv()
                got = rs_in[h, group.slot(h, stage - 1, piece)].astype(F32)
                part[h, piece] = part[h, piece] + got

    for load in loads[4:]:
        load.wait()
    in_scale = scale_rows(ideg_ref, me_r * (rows // TILE))
    last = group.stages - 1
    totals = []
    for h in range(2):
        rs_copy(h, last, me_r).wait_recv()
        got = rs_in[h, group.slot(h, last, me_r)].astype(F32)
        totals.append(((part[h, me_r] + got) * in_scale).astype(BF16))
    agg = jnp.concatenate(totals, axis=1)
    pre_act = jnp.dot(agg, w_ref[...], preferred_element_type=F32)
    gate = jax.nn.sigmoid(pre_act)
    hid_ref[...] = (pre_act * gate).astype(BF16)
    store_hid = pltpu.make_async_copy(hid_ref, hid_hbm, out_sem.at[0])
    store_hid.start()
    slope = gate * (1.0 + pre_act * (1.0 - gate))
    pre_grad = (cot_ref[...].astype(F32) * slope).astype(BF16)
    back = lax.dot_general(
        pre_grad, w_ref[...], (((1,), (1,)), ((), ())), preferred_element_type=F32
    )

    def ag_copy(h, stage, piece):
        slot = group.slot(h, stage, piece)
        return remote(
            tg.at[h, piece], tg.at[h, piece], ag_send.at[h, slot], ag_recv.at[h, slot],
            row_id(group.partner(group.orders[h][stage])),
        )

    for h in range(2):
        tg[h, me_r] = (back[:, h * half_w:(h + 1) * half_w] * in_scale).astype(BF16)
        for stage in reversed(range(group.stages)):
            ag_copy(h, stage, me_r).start()

    wg_part = lax.dot_general(
        agg, pre_grad, (((0,), (0,)), ((), ())), preferred_element_type=F32
    )
    piece_rows = hid // nr
    wga_out[...] = wg_part.astype(BF16).reshape(nr, piece_rows, hid)

    def wa_copy(d):
        to = lax.rem(me_r + d, nr)
        return remote(
            wga_out.at[to], wga_in.at[d], wa_send.at[d], wa_recv.at[d], row_id(to)
        )

    def wb_copy(d):
        to = lax.rem(me_c + d, nc)
        return remote(
            wgb_in.at[me_c], wgb_in.at[me_c], wb_send.at[d], wb_recv.at[d], col_id(to)
        )

    def wb_arrival(d):
        frm = lax.rem(me_c + nc - d, nc)
        return remote(
            wgb_in.at[frm], wgb_in.at[frm], wb_send.at[d], wb_recv.at[d],
            col_id(lax.rem(me_c + d, nc)),
        )

    def wc_copy(d):
        to = lax.rem(me_r + d, nr)
        return remote(
            wgc_in.at[me_r], wgc_in.at[me_r], wc_send.at[d], wc_recv.at[d], row_id(to)
        )

    def wc_arrival(d):
        frm = lax.rem(me_r + nr - d, nr)
        return remote(
            wgc_in.at[frm], wgc_in.at[frm], wc_send.at[d], wc_recv.at[d],
            row_id(lax.rem(me_r + d, nr)),
        )

    def ag_receive(h, stage, piece):
        ag_copy(h, stage, piece).wait_recv()
        for onward in reversed(range(stage)):
            ag_copy(h, onward, piece).start()

    for stage in reversed(range(1, group.stages)):
        for h in range(2):
            for piece in group.pieces(h, stage, False):
                ag_receive(h, stage, piece)

    for d in range(1, nr):
        wa_copy(d).start()

    for h in range(2):
        for piece in group.pieces(h, 0, False):
            ag_receive(h, 0, piece)

    def zq_copy(h, hops, right):
        way, step = (0, 1) if right else (1, -1)
        dest = me_c + step * hops
        if hops <= 2:
            into, sem, to = zq_fin.at[way, hops - 1, h], zf_recv.at[way, hops - 1, h], dest
        else:
            into, sem, to = zq_in.at[way, h, dest], zq_recv.at[way, h, dest], me_c + step
        return remote(zq_out.at[h, dest], into, zq_send.at[h, dest], sem, col_id(to))

    def zq_relayed(h, dest, right):
        way = 0 if right else 1
        return remote(
            zq_out.at[h, dest], zq_in.at[way, h, dest], zq_send.at[h, dest],
            zq_recv.at[way, h, dest], col_id(dest),
        )

    def zq_final(h, hops, right):
        way = 0 if right else 1
        return remote(
            zq_out.at[h, me_c], zq_fin.at[way, hops - 1, h], zq_send.at[h, me_c],
            zf_recv.at[way, hops - 1, h], col_id(me_c + 1 if right else me_c - 1),
        )

    def source_sums(dest):
        at = pl.ds(pl.multiple_of(dest * rows, rows), rows)
        block = jnp.concatenate([adj_t[t, at, :] for t in range(tb)], axis=1)
        return [
            jnp.dot(block, tg[h].reshape(nr * rows, half_w), preferred_element_type=F32)
            for h in range(2)
        ]

    def stream(m, right):
        dest = me_c + m if right else me_c - m
        way = 0 if right else 1

        @pl.when(inside(m, right))
        def _():
            sums = source_sums(dest)
            for h in range(2):
                zq_out[h, dest] = sums[h].astype(BF16)
                if m >= 2:
                    @pl.when(inside(1, not right))
                    def _():
                        zq_relayed(h, dest, right).wait_recv()
                        got = zq_in[way, h, dest].astype(F32)
                        zq_out[h, dest] = (sums[h] + got).astype(BF16)

                zq_copy(h, m, right).start()

    for m in range(nc - 1, 2, -1):
        for right in (True, False):
            stream(m, right)
    for right in (True, False):
        stream(1, right)

    for d in range(1, nr):
        wa_copy(d).wait_recv()
    own = wga_out[me_r].astype(F32)
    for d in range(1, nr):
        own = own + wga_in[d].astype(F32)
    wgb_in[me_c] = own
    for d in range(1, nc):
        wb_copy(d).start()

    for right in (True, False):
        stream(2, right)

    own_sums = source_sums(me_c)
    for h in range(2):
        part[h, 0] = own_sums[h]

    for d in range(1, nc):
        wb_arrival(d).wait_recv()
    total = wgb_in[0]
    for c in range(1, nc):
        total = total + wgb_in[c]
    wgc_in[me_r] = total
    for d in range(1, nr):
        wc_copy(d).start()

    for hops in (1, 2):
        for h in range(2):
            for right in (True, False):
                way = 0 if right else 1

                @pl.when(inside(hops, not right))
                def _():
                    zq_final(h, hops, right).wait_recv()
                    part[h, 0] = part[h, 0] + zq_fin[way, hops - 1, h].astype(F32)

    for h in range(2):
        ig_ref[:, h * half_w:(h + 1) * half_w] = (part[h, 0] * out_scale).astype(BF16)
    store_ig = pltpu.make_async_copy(ig_ref, ig_hbm, out_sem.at[1])
    store_ig.start()

    for d in range(1, nr):
        wc_arrival(d).wait_recv()
    store_wg = pltpu.make_async_copy(wgc_in, wg_hbm, out_sem.at[2])
    store_wg.start()

    for h in range(2):
        gather_own(h, lambda c: c.wait_send())
        for k in range(2, nc):
            gather_onward(h, k, lambda c: c.wait_send())
        for stage in range(group.stages):
            for piece in group.pieces(h, stage, False):
                rs_copy(h, stage, piece).wait_send()
            for piece in group.pieces(h, stage, True):
                ag_copy(h, stage, piece).wait_send()
        for m in range(1, nc):
            for right in (True, False):
                @pl.when(inside(m, right))
                def _():
                    zq_copy(h, m, right).wait_send()
    for d in range(1, nr):
        wa_copy(d).wait_send()
        wc_copy(d).wait_send()
    for d in range(1, nc):
        wb_copy(d).wait_send()
    store_hid.wait()
    store_ig.wait()
    store_wg.wait()


def place(hid_in, ig_in, wg_in, hid_out, ig_out, wg_out):
    hid_out[...] = hid_in[...]
    ig_out[...] = ig_in[...]
    wg_out[...] = wg_in[...]


def shards(
    nr, nc,
    features, out_degree, in_degree, tile_blocks, tile_count, tile_weights, weight, cotangent
):
    rows, hid = features.shape
    half_w = hid // 2
    slots = tile_weights.shape[2]
    src_rows, tgt_rows = out_degree.shape[0], in_degree.shape[0]
    sb, tb = src_rows // TILE, tgt_rows // TILE
    anywhere = pl.BlockSpec(memory_space=pl.ANY)
    dma = pltpu.SemaphoreType.DMA
    table_rows = -(-sb * tb // slots)
    out_shape = (
        jax.ShapeDtypeStruct((rows, hid), BF16),
        jax.ShapeDtypeStruct((rows, hid), BF16),
        jax.ShapeDtypeStruct((nr, hid // nr, hid), F32),
    )
    results = pl.pallas_call(
        functools.partial(kernel, nr, nc),
        out_shape=out_shape,
        in_specs=[anywhere] * 8,
        out_specs=(anywhere,) * 3,
        scratch_shapes=[
            pltpu.VMEM((rows, hid), BF16),
            pltpu.VMEM((sb, TILE), jnp.int32),
            pltpu.VMEM((tb, TILE), jnp.int32),
            pltpu.VMEM((2, slots), jnp.int32),
            pltpu.VMEM((1, 1), jnp.int32),
            pltpu.VMEM((hid, hid), BF16),
            pltpu.VMEM((rows, hid), BF16),
            pltpu.VMEM((rows, hid), BF16),
            pltpu.VMEM((rows, hid), BF16),
            dma((7,)), dma((3,)),
            pltpu.VMEM((slots, TILE, TILE), BF16),
            pltpu.VMEM((tgt_rows, src_rows), BF16),
            pltpu.VMEM((tb, src_rows, TILE), BF16),
            pltpu.VMEM((table_rows, slots), jnp.int32),
            pltpu.SMEM((table_rows, slots), jnp.int32),
            pltpu.VMEM((2, nc, rows, half_w), BF16),
            pltpu.VMEM((2, nr, rows, half_w), F32),
            pltpu.VMEM((2, nr, rows, half_w), BF16),
            pltpu.VMEM((2, nr - 1, rows, half_w), BF16),
            pltpu.VMEM((2, nr, rows, half_w), BF16),
            pltpu.VMEM((2, nc, rows, half_w), BF16),
            pltpu.VMEM((2, 2, nc, rows, half_w), BF16),
            pltpu.VMEM((2, 2, 2, rows, half_w), BF16),
            pltpu.VMEM((nr, hid // nr, hid), BF16),
            pltpu.VMEM((nr, hid // nr, hid), BF16),
            pltpu.VMEM((nc, hid // nr, hid), F32),
            pltpu.VMEM((nr, hid // nr, hid), F32),
            dma, dma,
            dma((2, 2, nc)), dma((2, nc)),
            dma((2, nr - 1)), dma((2, nr - 1)),
            dma((2, nr - 1)), dma((2, nr - 1)),
            dma((2, nc)), dma((2, 2, nc)), dma((2, 2, 2)),
            dma((nr,)), dma((nr,)),
            dma((nc,)), dma((nc,)),
            dma((nr,)), dma((nr,)),
        ],
        compiler_params=pltpu.CompilerParams(
            collective_id=0, has_side_effects=True, vmem_limit_bytes=60 * 1024 * 1024
        ),
    )(
        features,
        out_degree.reshape(sb, TILE),
        in_degree.reshape(tb, TILE),
        tile_blocks[0, 0],
        tile_count,
        tile_weights[0, 0],
        weight,
        cotangent,
    )
    hidden, input_grad, weight_grad = pl.pallas_call(
        place,
        out_shape=out_shape,
        in_specs=[pl.BlockSpec(memory_space=pltpu.VMEM)] * 3,
        out_specs=(pl.BlockSpec(memory_space=pltpu.VMEM),) * 3,
    )(*results)
    return hidden, input_grad, weight_grad.reshape(hid, hid)


def solution(mesh):
    nr, nc = mesh.shape["row"], mesh.shape["col"]
    placed = (
        P(("row", "col"), None),
        P("row"),
        P("col"),
        P("row", "col", None, None),
        P("row", "col"),
        P("row", "col", None, None, None),
        P(),
        P(("col", "row"), None),
    )
    return jax.shard_map(
        functools.partial(shards, nr, nc),
        mesh=mesh,
        in_specs=placed,
        out_specs=(P(("col", "row"), None), P(("row", "col"), None), P()),
        check_vma=False,
    )
```

```python
import functools

import jax
import jax.numpy as jnp
from jax import lax
from jax.experimental import pallas as pl
from jax.experimental.pallas import tpu as pltpu
from jax.sharding import PartitionSpec as P

TILE = 128
F32 = jnp.float32
BF16 = jnp.bfloat16
MESH = pl.DeviceIdType.MESH


def bit_orders(nr):
    bits = nr.bit_length() - 1
    return ([0] + list(range(1, bits)), [0] + list(range(bits - 1, 0, -1)))


class Group:
    def __init__(self, nr, me):
        self.nr, self.me = nr, me
        self.orders = bit_orders(nr)
        self.stages = len(self.orders[0])
        self.base = [nr - (nr >> s) for s in range(self.stages)]

    def bit(self, value, k):
        return (value // (1 << k)) % 2

    def partner(self, k):
        return self.me + (1 << k) * (1 - 2 * self.bit(self.me, k))

    def slot(self, half, stage, piece):
        rest = self.orders[half][stage + 1:]
        return self.base[stage] + sum(
            (self.bit(piece, b) * (1 << i) for i, b in enumerate(rest)), 0
        )

    def pieces(self, half, stage, mine, near_first=False):
        order = self.orders[half]
        own = sum((self.bit(self.me, b) * (1 << b) for b in order[:stage]), 0)
        k = order[stage]
        here = self.bit(self.me, k)
        here = here if mine else 1 - here
        rest = order[stage + 1:]
        return [
            own + here * (1 << k) + sum(
                ((self.bit(self.me, b) + (j >> i) % 2) % 2 * (1 << b) for i, b in enumerate(rest)),
                0,
            )
            for j in (range(1 << len(rest)) if near_first else reversed(range(1 << len(rest))))
        ]


def kernel(
    nr, nc,
    feat_hbm, odeg_hbm, ideg_hbm, blocks_hbm, count_hbm, tiles_hbm, w_hbm, cot_hbm,
    hid_hbm, ig_hbm, wg_hbm,
    feat_ref, odeg_ref, ideg_ref, blocks_ref, count_ref, w_ref, cot_ref, hid_ref, ig_ref,
    in_sem, out_sem,
    tiles, adj, adj_t, table_v, table_s, src, part, rs_out, rs_in, tg, zq_out, zq_in, zq_fin,
    wga_out, wga_in, wgb_in, wgc_in,
    loc_sem, tab_sem, zs_send, zs_recv, rs_send, rs_recv, ag_send, ag_recv,
    zq_send, zq_recv, zf_recv, wa_send, wa_recv, wb_send, wb_recv, wc_send, wc_recv,
):
    rows, hid = feat_ref.shape
    half_w = hid // 2
    sb, tb = nc * rows // TILE, nr * rows // TILE
    slots = tiles.shape[0]
    me_r, me_c = lax.axis_index("row"), lax.axis_index("col")
    group = Group(nr, me_r)
    row_id = lambda r: {"row": r, "col": me_c}
    col_id = lambda c: {"row": me_r, "col": c}

    def remote(src_ref, dst_ref, send, recv, where):
        return pltpu.make_async_remote_copy(
            src_ref=src_ref, dst_ref=dst_ref, send_sem=send, recv_sem=recv,
            device_id=where, device_id_type=MESH,
        )

    barrier = pltpu.get_barrier_semaphore()
    for d in range(1, nr):
        pl.semaphore_signal(
            barrier, inc=1, device_id=row_id(lax.rem(me_r + d, nr)), device_id_type=MESH
        )
    for d in range(1, nc):
        pl.semaphore_signal(
            barrier, inc=1, device_id=col_id(lax.rem(me_c + d, nc)), device_id_type=MESH
        )

    loads = [
        pltpu.make_async_copy(a, b, in_sem.at[i])
        for i, (a, b) in enumerate([
            (feat_hbm, feat_ref), (odeg_hbm, odeg_ref), (blocks_hbm, blocks_ref),
            (count_hbm, count_ref), (ideg_hbm, ideg_ref), (w_hbm, w_ref), (cot_hbm, cot_ref),
        ])
    ]
    load_tiles = pltpu.make_async_copy(tiles_hbm, tiles, loc_sem)
    for load in loads:
        load.start()
    load_tiles.start()
    loads[0].wait()
    loads[1].wait()

    def scale_rows(deg_ref, first):
        cols = []
        for h in range(rows // TILE):
            deg = deg_ref[pl.ds(first + h, 1), :]
            line = lax.rsqrt(deg.astype(F32))
            cols.append(jnp.broadcast_to(line, (TILE, TILE)).T)
        return jnp.concatenate(cols, axis=0)

    out_scale = scale_rows(odeg_ref, me_c * (rows // TILE))
    for h in range(2):
        cut = slice(h * half_w, (h + 1) * half_w)
        src[h, me_c] = (feat_ref[:, cut].astype(F32) * out_scale).astype(BF16)

    pl.semaphore_wait(barrier, nr + nc - 2)

    def gather_copy(h, block, hops, right, at):
        to = me_c + hops if right else me_c - hops
        return remote(
            src.at[h, block], src.at[h, block],
            zs_send.at[0 if right else 1, h, at], zs_recv.at[h, block], col_id(to),
        )

    def inside(step, right):
        return me_c + step < nc if right else me_c >= step

    def gather_own(h, act):
        for hops in (2, 1):
            for right in (True, False):
                @pl.when(inside(hops, right))
                def _():
                    act(gather_copy(h, me_c, hops, right, hops - 1))

    def gather_onward(h, k, act):
        for right in (True, False):
            @pl.when(jnp.logical_and(inside(k, not right), inside(1, right)))
            def _():
                act(gather_copy(h, me_c - k if right else me_c + k, 1, right, k))

    def gather_arrived(h, k):
        for right in (True, False):
            @pl.when(inside(k, not right))
            def _():
                gather_copy(h, me_c - k if right else me_c + k, 1, right, k).wait_recv()

    for h in range(2):
        gather_own(h, lambda c: c.start())

    loads[2].wait()
    loads[3].wait()
    flat = blocks_ref[0:1, :] * sb + blocks_ref[1:2, :]
    slot_line = lax.broadcasted_iota(jnp.int32, (1, slots), 1)
    flat = jnp.where(slot_line < count_ref[...], flat, -1)
    down = jnp.broadcast_to(flat.astype(F32), (slots, slots)).T.astype(jnp.int32)
    slot_down = lax.broadcasted_iota(jnp.int32, (slots, slots), 0)
    lane = lax.broadcasted_iota(jnp.int32, (slots, slots), 1)
    for g in range(table_v.shape[0]):
        found = jnp.where(down == lane + g * slots, slot_down, -1)
        table_v[g:g + 1, :] = jnp.max(found, axis=0, keepdims=True)
    to_smem = pltpu.make_async_copy(table_v, table_s, tab_sem)
    to_smem.start()
    to_smem.wait()
    load_tiles.wait()

    def densify(t, carry):
        for s in range(sb):
            at = t * sb + s
            slot = table_s[at // slots, at % slots]
            tile = tiles[jnp.maximum(slot, 0)]
            tile = jnp.where(slot >= 0, tile, jnp.zeros_like(tile))
            adj[pl.ds(t * TILE, TILE), s * TILE:(s + 1) * TILE] = tile
            adj_t[t, s * TILE:(s + 1) * TILE, :] = tile.T
        return carry

    lax.fori_loop(0, tb, densify, 0)

    for k in range(2, nc):
        for h in range(2):
            gather_arrived(h, k)
            gather_onward(h, k, lambda c: c.start())
    for h in range(2):
        gather_arrived(h, 1)

    def rs_copy(h, stage, piece):
        slot = group.slot(h, stage, piece)
        return remote(
            rs_out.at[h, piece], rs_in.at[h, slot], rs_send.at[h, slot], rs_recv.at[h, slot],
            row_id(group.partner(group.orders[h][stage])),
        )

    def both_halves(block, held, depth):
        full = jnp.concatenate([held[h].reshape(depth, half_w) for h in range(2)], axis=1)
        sums = jnp.dot(block, full, preferred_element_type=F32)
        return [sums[:, h * half_w:(h + 1) * half_w] for h in range(2)]

    def target_sums(piece):
        block = adj[pl.ds(pl.multiple_of(piece * rows, rows), rows), :]
        return both_halves(block, src, nc * rows)

    for piece in group.pieces(0, 0, False):
        sums = target_sums(piece)
        for h in range(2):
            rs_out[h, piece] = sums[h].astype(BF16)
            rs_copy(h, 0, piece).start()
    for piece in group.pieces(0, 0, True):
        sums = target_sums(piece)
        for h in range(2):
            part[h, piece] = sums[h]

    for stage in range(1, group.stages):
        for h in range(2):
            for piece in group.pieces(h, stage, False):
                rs_copy(h, stage - 1, piece).wait_recv()
                got = rs_in[h, group.slot(h, stage - 1, piece)].astype(F32)
                rs_out[h, piece] = (part[h, piece] + got).astype(BF16)
                rs_copy(h, stage, piece).start()
        for h in range(2):
            for piece in group.pieces(h, stage, True):
                rs_copy(h, stage - 1, piece).wait_recv()
                got = rs_in[h, group.slot(h, stage - 1, piece)].astype(F32)
                part[h, piece] = part[h, piece] + got

    for load in loads[4:]:
        load.wait()
    in_scale = scale_rows(ideg_ref, me_r * (rows // TILE))
    last = group.stages - 1
    totals = []
    for h in range(2):
        rs_copy(h, last, me_r).wait_recv()
        got = rs_in[h, group.slot(h, last, me_r)].astype(F32)
        totals.append(((part[h, me_r] + got) * in_scale).astype(BF16))
    agg = jnp.concatenate(totals, axis=1)
    pre_act = jnp.dot(agg, w_ref[...], preferred_element_type=F32)
    gate = jax.nn.sigmoid(pre_act)
    hid_ref[...] = (pre_act * gate).astype(BF16)
    store_hid = pltpu.make_async_copy(hid_ref, hid_hbm, out_sem.at[0])
    store_hid.start()
    slope = gate * (1.0 + pre_act * (1.0 - gate))
    pre_grad = (cot_ref[...].astype(F32) * slope).astype(BF16)
    back = lax.dot_general(
        pre_grad, w_ref[...], (((1,), (1,)), ((), ())), preferred_element_type=F32
    )

    def ag_copy(h, stage, piece):
        slot = group.slot(h, stage, piece)
        return remote(
            tg.at[h, piece], tg.at[h, piece], ag_send.at[h, slot], ag_recv.at[h, slot],
            row_id(group.partner(group.orders[h][stage])),
        )

    for h in range(2):
        tg[h, me_r] = (back[:, h * half_w:(h + 1) * half_w] * in_scale).astype(BF16)
        for stage in reversed(range(group.stages)):
            ag_copy(h, stage, me_r).start()

    wg_part = lax.dot_general(
        agg, pre_grad, (((0,), (0,)), ((), ())), preferred_element_type=F32
    )
    piece_rows = hid // nr
    wga_out[...] = wg_part.astype(BF16).reshape(nr, piece_rows, hid)

    def wa_copy(d):
        to = lax.rem(me_r + d, nr)
        return remote(
            wga_out.at[to], wga_in.at[d], wa_send.at[d], wa_recv.at[d], row_id(to)
        )

    def wb_copy(d):
        to = lax.rem(me_c + d, nc)
        return remote(
            wgb_in.at[me_c], wgb_in.at[me_c], wb_send.at[d], wb_recv.at[d], col_id(to)
        )

    def wb_arrival(d):
        frm = lax.rem(me_c + nc - d, nc)
        return remote(
            wgb_in.at[frm], wgb_in.at[frm], wb_send.at[d], wb_recv.at[d],
            col_id(lax.rem(me_c + d, nc)),
        )

    def wc_copy(d):
        to = lax.rem(me_r + d, nr)
        return remote(
            wgc_in.at[me_r], wgc_in.at[me_r], wc_send.at[d], wc_recv.at[d], row_id(to)
        )

    def wc_arrival(d):
        frm = lax.rem(me_r + nr - d, nr)
        return remote(
            wgc_in.at[frm], wgc_in.at[frm], wc_send.at[d], wc_recv.at[d],
            row_id(lax.rem(me_r + d, nr)),
        )

    def ag_receive(h, stage, piece):
        ag_copy(h, stage, piece).wait_recv()
        for onward in reversed(range(stage)):
            ag_copy(h, onward, piece).start()

    for stage in reversed(range(1, group.stages)):
        for h in range(2):
            for piece in group.pieces(h, stage, False, near_first=True):
                ag_receive(h, stage, piece)

    for d in range(1, nr):
        wa_copy(d).start()

    for h in range(2):
        for piece in group.pieces(h, 0, False, near_first=True):
            ag_receive(h, 0, piece)

    def zq_copy(h, hops, right):
        way, step = (0, 1) if right else (1, -1)
        dest = me_c + step * hops
        if hops <= 2:
            into, sem, to = zq_fin.at[way, hops - 1, h], zf_recv.at[way, hops - 1, h], dest
        else:
            into, sem, to = zq_in.at[way, h, dest], zq_recv.at[way, h, dest], me_c + step
        return remote(zq_out.at[h, dest], into, zq_send.at[h, dest], sem, col_id(to))

    def zq_relayed(h, dest, right):
        way = 0 if right else 1
        return remote(
            zq_out.at[h, dest], zq_in.at[way, h, dest], zq_send.at[h, dest],
            zq_recv.at[way, h, dest], col_id(dest),
        )

    def zq_final(h, hops, right):
        way = 0 if right else 1
        return remote(
            zq_out.at[h, me_c], zq_fin.at[way, hops - 1, h], zq_send.at[h, me_c],
            zf_recv.at[way, hops - 1, h], col_id(me_c + 1 if right else me_c - 1),
        )

    def source_sums(dest):
        at = pl.ds(pl.multiple_of(dest * rows, rows), rows)
        block = jnp.concatenate([adj_t[t, at, :] for t in range(tb)], axis=1)
        return both_halves(block, tg, nr * rows)

    def stream(m, right):
        dest = me_c + m if right else me_c - m
        way = 0 if right else 1

        @pl.when(inside(m, right))
        def _():
            sums = source_sums(dest)
            for h in range(2):
                zq_out[h, dest] = sums[h].astype(BF16)
                if m >= 2:
                    @pl.when(inside(1, not right))
                    def _():
                        zq_relayed(h, dest, right).wait_recv()
                        got = zq_in[way, h, dest].astype(F32)
                        zq_out[h, dest] = (sums[h] + got).astype(BF16)

                zq_copy(h, m, right).start()

    for m in range(nc - 1, 2, -1):
        for right in (True, False):
            stream(m, right)
    for right in (True, False):
        stream(1, right)

    for d in range(1, nr):
        wa_copy(d).wait_recv()
    own = wga_out[me_r].astype(F32)
    for d in range(1, nr):
        own = own + wga_in[d].astype(F32)
    wgb_in[me_c] = own
    for d in range(1, nc):
        wb_copy(d).start()

    for right in (True, False):
        stream(2, right)

    own_sums = source_sums(me_c)
    for h in range(2):
        part[h, 0] = own_sums[h]

    for d in range(1, nc):
        wb_arrival(d).wait_recv()
    total = wgb_in[0]
    for c in range(1, nc):
        total = total + wgb_in[c]
    wgc_in[me_r] = total
    for d in range(1, nr):
        wc_copy(d).start()

    for hops in (1, 2):
        for h in range(2):
            for right in (True, False):
                way = 0 if right else 1

                @pl.when(inside(hops, not right))
                def _():
                    zq_final(h, hops, right).wait_recv()
                    part[h, 0] = part[h, 0] + zq_fin[way, hops - 1, h].astype(F32)

    for h in range(2):
        ig_ref[:, h * half_w:(h + 1) * half_w] = (part[h, 0] * out_scale).astype(BF16)
    store_ig = pltpu.make_async_copy(ig_ref, ig_hbm, out_sem.at[1])
    store_ig.start()

    for d in range(1, nr):
        wc_arrival(d).wait_recv()
    store_wg = pltpu.make_async_copy(wgc_in, wg_hbm, out_sem.at[2])
    store_wg.start()

    for h in range(2):
        gather_own(h, lambda c: c.wait_send())
        for k in range(2, nc):
            gather_onward(h, k, lambda c: c.wait_send())
        for stage in range(group.stages):
            for piece in group.pieces(h, stage, False):
                rs_copy(h, stage, piece).wait_send()
            for piece in group.pieces(h, stage, True):
                ag_copy(h, stage, piece).wait_send()
        for m in range(1, nc):
            for right in (True, False):
                @pl.when(inside(m, right))
                def _():
                    zq_copy(h, m, right).wait_send()
    for d in range(1, nr):
        wa_copy(d).wait_send()
        wc_copy(d).wait_send()
    for d in range(1, nc):
        wb_copy(d).wait_send()
    store_hid.wait()
    store_ig.wait()
    store_wg.wait()


def place(hid_in, ig_in, wg_in, hid_out, ig_out, wg_out):
    hid_out[...] = hid_in[...]
    ig_out[...] = ig_in[...]
    wg_out[...] = wg_in[...]


def shards(
    nr, nc,
    features, out_degree, in_degree, tile_blocks, tile_count, tile_weights, weight, cotangent
):
    rows, hid = features.shape
    half_w = hid // 2
    slots = tile_weights.shape[2]
    src_rows, tgt_rows = out_degree.shape[0], in_degree.shape[0]
    sb, tb = src_rows // TILE, tgt_rows // TILE
    anywhere = pl.BlockSpec(memory_space=pl.ANY)
    dma = pltpu.SemaphoreType.DMA
    table_rows = -(-sb * tb // slots)
    out_shape = (
        jax.ShapeDtypeStruct((rows, hid), BF16),
        jax.ShapeDtypeStruct((rows, hid), BF16),
        jax.ShapeDtypeStruct((nr, hid // nr, hid), F32),
    )
    results = pl.pallas_call(
        functools.partial(kernel, nr, nc),
        out_shape=out_shape,
        in_specs=[anywhere] * 8,
        out_specs=(anywhere,) * 3,
        scratch_shapes=[
            pltpu.VMEM((rows, hid), BF16),
            pltpu.VMEM((sb, TILE), jnp.int32),
            pltpu.VMEM((tb, TILE), jnp.int32),
            pltpu.VMEM((2, slots), jnp.int32),
            pltpu.VMEM((1, 1), jnp.int32),
            pltpu.VMEM((hid, hid), BF16),
            pltpu.VMEM((rows, hid), BF16),
            pltpu.VMEM((rows, hid), BF16),
            pltpu.VMEM((rows, hid), BF16),
            dma((7,)), dma((3,)),
            pltpu.VMEM((slots, TILE, TILE), BF16),
            pltpu.VMEM((tgt_rows, src_rows), BF16),
            pltpu.VMEM((tb, src_rows, TILE), BF16),
            pltpu.VMEM((table_rows, slots), jnp.int32),
            pltpu.SMEM((table_rows, slots), jnp.int32),
            pltpu.VMEM((2, nc, rows, half_w), BF16),
            pltpu.VMEM((2, nr, rows, half_w), F32),
            pltpu.VMEM((2, nr, rows, half_w), BF16),
            pltpu.VMEM((2, nr - 1, rows, half_w), BF16),
            pltpu.VMEM((2, nr, rows, half_w), BF16),
            pltpu.VMEM((2, nc, rows, half_w), BF16),
            pltpu.VMEM((2, 2, nc, rows, half_w), BF16),
            pltpu.VMEM((2, 2, 2, rows, half_w), BF16),
            pltpu.VMEM((nr, hid // nr, hid), BF16),
            pltpu.VMEM((nr, hid // nr, hid), BF16),
            pltpu.VMEM((nc, hid // nr, hid), F32),
            pltpu.VMEM((nr, hid // nr, hid), F32),
            dma, dma,
            dma((2, 2, nc)), dma((2, nc)),
            dma((2, nr - 1)), dma((2, nr - 1)),
            dma((2, nr - 1)), dma((2, nr - 1)),
            dma((2, nc)), dma((2, 2, nc)), dma((2, 2, 2)),
            dma((nr,)), dma((nr,)),
            dma((nc,)), dma((nc,)),
            dma((nr,)), dma((nr,)),
        ],
        compiler_params=pltpu.CompilerParams(
            collective_id=0, has_side_effects=True, vmem_limit_bytes=60 * 1024 * 1024
        ),
    )(
        features,
        out_degree.reshape(sb, TILE),
        in_degree.reshape(tb, TILE),
        tile_blocks[0, 0],
        tile_count,
        tile_weights[0, 0],
        weight,
        cotangent,
    )
    hidden, input_grad, weight_grad = pl.pallas_call(
        place,
        out_shape=out_shape,
        in_specs=[pl.BlockSpec(memory_space=pltpu.VMEM)] * 3,
        out_specs=(pl.BlockSpec(memory_space=pltpu.VMEM),) * 3,
    )(*results)
    return hidden, input_grad, weight_grad.reshape(hid, hid)


def solution(mesh):
    nr, nc = mesh.shape["row"], mesh.shape["col"]
    placed = (
        P(("row", "col"), None),
        P("row"),
        P("col"),
        P("row", "col", None, None),
        P("row", "col"),
        P("row", "col", None, None, None),
        P(),
        P(("col", "row"), None),
    )
    return jax.shard_map(
        functools.partial(shards, nr, nc),
        mesh=mesh,
        in_specs=placed,
        out_specs=(P(("col", "row"), None), P(("row", "col"), None), P()),
        check_vma=False,
    )
```
